256 devices in a mesh: row: 16 (over z_lo, y, core), col: 16 (over z_hi, x).
Axes of the slice: x: 4, y: 4, z: 8 (z_hi: 4, z_lo: 2; z = z_hi * 2 + z_lo), core: 2. Of those that a mesh axis runs over, the one named last changes fastest.
Arguments:
- cov: float32 [16384, 16384], P('row', 'col'), may hold values from -40 to 40, as said below
- noise: float32 [16384, 16384], P('row', 'col'), may hold values from -12 to 12, as said below
- velocity_x: float32 [128, 128], replicated, may hold values from -0.8 to 0.8
- velocity_y: float32 [128, 128], replicated, may hold values from -0.8 to 0.8
- diffusion: float32 [128, 128], replicated, may hold values from 0.05 to 0.25
Outputs:
- forecast: float32 [16384, 16384], P('row', 'col')
The draws below stay inside these ranges and needn't reach their ends.
Inputs may be any that keep to these rules, and one draw needn't show every extreme that they name: `cov`: symmetric, its diagonal lifted by 2. `noise`: symmetric, its diagonal lifted by 0.5.
All inputs are finite; a program needn't handle non-finite values.
Results may differ from the reference program's by a relative error of at most 0.000061.
Values sent between devices are 32-bit elements; how exact they have to be, the bound alone decides.
A program may use at most 64 MiB of HBM per device.

```python
import math
import jax
import jax.numpy as jnp
from jax import lax

NLAT = 128
NLON = 128
N = 16384


def symmetric_draw(key, scale, lift):
    base = jax.random.truncated_normal(key, -4.0, 4.0, (N, N), jnp.float32)
    sym = (base + base.T) * (0.5 * scale)
    return sym + lift * jnp.eye(N, dtype=jnp.float32)


def draw_cov(key, part):
    return symmetric_draw(jax.random.fold_in(key, 11), 1.0, 2.0)


def draw_noise(key, part):
    return symmetric_draw(jax.random.fold_in(key, 23), 0.3, 0.5)


def setup_inputs(seed: int = 0) -> dict:
    arg_keys = jax.random.split(jax.random.key(seed), 6)
    return {
        "cov": draw_cov(jax.random.fold_in(arg_keys[5], 71), 0),
        "noise": draw_noise(jax.random.fold_in(arg_keys[5], 71), 0),
        "velocity_x": jnp.clip(jax.random.uniform(arg_keys[2], (NLAT, NLON), jnp.float32, -0.8, 0.8), -0.8, 0.8),
        "velocity_y": jnp.clip(jax.random.uniform(arg_keys[3], (NLAT, NLON), jnp.float32, -0.8, 0.8), -0.8, 0.8),
        "diffusion": jnp.clip(jnp.exp(jax.random.uniform(arg_keys[4], (NLAT, NLON), jnp.float32, math.log(0.05), math.log(0.25))), 0.05, 0.25),
    }


third = 1.0 / 3.0
two_thirds = 2.0 / 3.0


def tendency(extended, kappa, vel_x, vel_y, axis):
    rows = extended.shape[axis] - 2
    centre = lax.slice_in_dim(extended, 1, rows + 1, axis=axis)
    north = lax.slice_in_dim(extended, 2, rows + 2, axis=axis)
    south = lax.slice_in_dim(extended, 0, rows, axis=axis)
    east = jnp.roll(centre, -1, axis + 1)
    west = jnp.roll(centre, 1, axis + 1)
    return kappa * (east + west + north + south - 4.0 * centre) - 0.5 * vel_x * (east - west) - 0.5 * vel_y * (north - south)


def apply_step(field, kappa, vel_x, vel_y, axis):
    def padded(value):
        widths = [(0, 0)] * value.ndim
        widths[axis] = (1, 1)
        return jnp.pad(value, widths)

    first = field + tendency(padded(field), kappa, vel_x, vel_y, axis)
    second = 0.75 * field + 0.25 * (first + tendency(padded(first), kappa, vel_x, vel_y, axis))
    return third * field + two_thirds * (second + tendency(padded(second), kappa, vel_x, vel_y, axis))


def reference(cov, noise, velocity_x, velocity_y, diffusion):
    size = NLAT * NLON
    count = 16
    rows = size // count

    def along_last(block):
        shaped = block.reshape(rows, NLAT, NLON)
        return apply_step(shaped, diffusion, velocity_x, velocity_y, 1).reshape(rows, size)

    half = lax.map(along_last, cov.reshape(count, rows, size)).reshape(size, size)
    state = half.reshape(NLAT, NLON, size)

    def along_first(index):
        piece = lax.dynamic_slice_in_dim(state, index * rows, rows, 2)
        return apply_step(piece, diffusion[:, :, None], velocity_x[:, :, None], velocity_y[:, :, None], 0)

    blocks = lax.map(along_first, jnp.arange(count, dtype=jnp.int32))
    full = jnp.moveaxis(blocks, 0, 2).reshape(size, size)
    return full + noise
```

```python
import jax
import jax.numpy as jnp
from jax import lax
from jax.experimental import pallas as pl
from jax.experimental.pallas import tpu as pltpu
from jax.sharding import PartitionSpec as P

LATS = 8
GROUPS = 16
LON = 128
RIM = 3
WIDTH = LATS * LON
EDGE = RIM * LON
HALF_GROUPS = GROUPS // 2
QUARTER_GROUPS = GROUPS // 4
THIRD = 1.0 / 3.0


def combine(centre, north, south, east, west, coefs):
    c_east, c_west, c_north, c_south, c_centre = coefs
    return (
        (c_east * east + c_west * west)
        + (c_north * north + c_south * south)
        + c_centre * centre
    )


def coefficients(kappa, half_x, half_y):
    return (kappa - half_x, kappa + half_x, kappa - half_y, kappa + half_y, -4.0 * kappa)


def kernel(
    cov, noise, vel_x, vel_y, diffusion, out,
    ext, one, two, half, rows_coef, cols_coef, relay_x, relay_y,
    load_sem, send_x, recv_x, send_y, recv_y, relay_x_recv, relay_x_send, relay_y_recv, relay_y_send,
):
    row, col = lax.axis_index("row"), lax.axis_index("col")
    pos_x, z_hi = col % 4, col // 4
    first_x, last_x = pos_x == 0, pos_x == 3
    wrap_up = last_x & (col < 15)
    wrap_down = first_x & (col > 0)
    relay_up = first_x & (z_hi < 3)
    relay_down = last_x & (z_hi > 0)
    low_relay = (row == 0) | (row == 2) | (row == 4)
    high_relay = (row == 11) | (row == 13) | (row == 15)

    def at(r, c):
        return {"row": r, "col": c}

    barrier = pltpu.get_barrier_semaphore()
    greeted = jnp.int32(0)
    peers = [
        (row > 0, row - 1, col), (row < 15, row + 1, col), (col > 0, row, col - 1), (col < 15, row, col + 1),
        (first_x, row, col + 3), (last_x, row, col - 3),
        ((first_x | last_x) & (z_hi < 3), row, col + 4), ((first_x | last_x) & (z_hi > 0), row, col - 4),
        (low_relay | high_relay, 7, col), (low_relay | high_relay, 8, col),
    ]
    for other in (0, 2, 4, 11, 13, 15):
        peers.append(((row == 7) | (row == 8), other, col))
    for cond, r, c in peers:
        @pl.when(cond)
        def _(r=r, c=c):
            pl.semaphore_signal(barrier, 1, device_id=at(r, c))

        greeted = greeted + cond.astype(jnp.int32)

    load = pltpu.make_async_copy(cov, ext.at[RIM : RIM + LATS], load_sem.at[0])
    load.start()
    load_noise = pltpu.make_async_copy(noise, out, load_sem.at[1])
    load_noise.start()

    def build(i, _):
        def fields(lat):
            valid = ((lat >= 0) & (lat < 128)).astype(jnp.float32)
            lat = jnp.clip(lat, 0, 127)
            pick = pl.ds(lat, 1)
            return diffusion[pick, :] * valid, vel_x[pick, :] * (0.5 * valid), vel_y[pick, :] * (0.5 * valid)

        wide = [jnp.broadcast_to(f, (8, LON)) for f in fields(col * LATS - 2 + i)]
        for n, value in enumerate(coefficients(*wide)):
            cols_coef[n, i] = value
        tall = [jnp.broadcast_to(f, (LON, LON)).T for f in fields(row * LATS - 2 + i)]
        for n, value in enumerate(coefficients(*tall)):
            rows_coef[n, i] = value.reshape(GROUPS, 8, LON)
        return 0

    lax.fori_loop(0, LATS + 4, build, 0)

    @pl.when(row == 0)
    def _():
        ext[0:RIM] = jnp.zeros((RIM, GROUPS, 8, WIDTH), jnp.float32)

    @pl.when(row == 15)
    def _():
        ext[RIM + LATS :] = jnp.zeros((RIM, GROUPS, 8, WIDTH), jnp.float32)

    @pl.when(col == 0)
    def _():
        half[:, :, :, 0:EDGE] = jnp.zeros((LATS, GROUPS, 8, EDGE), jnp.float32)

    @pl.when(col == 15)
    def _():
        half[:, :, :, EDGE + WIDTH :] = jnp.zeros((LATS, GROUPS, 8, EDGE), jnp.float32)

    pl.semaphore_wait(barrier, greeted)

    def push(src, dst, send, recv, r, c):
        return pltpu.make_async_remote_copy(src, dst, send, recv, device_id=at(r, c))

    def row_copy(up, h, groups, r):
        lat, slot = (LATS - 1 - h, RIM - 1 - h) if up else (h, RIM + LATS + h)
        side = 0 if up else 1
        return push(cov.at[lat, groups], ext.at[slot, groups], send_y.at[side, h], recv_y.at[side, h], r, col)

    every = pl.ds(0, GROUPS)

    def quarter(i):
        return pl.ds(i * QUARTER_GROUPS, QUARTER_GROUPS)

    for h in range(RIM):
        @pl.when((row < 15) & (row != 7))
        def _():
            row_copy(True, h, every, row + 1).start()

        @pl.when((row > 0) & (row != 8))
        def _():
            row_copy(False, h, every, row - 1).start()

        @pl.when(row == 7)
        def _():
            for i in range(3):
                push(cov.at[LATS - 1 - h, quarter(i)], relay_y.at[h], send_y.at[0, h], relay_y_recv.at[h], 2 * i, col).start()
            row_copy(True, h, quarter(3), 8).start()

        @pl.when(row == 8)
        def _():
            for i in range(1, 4):
                push(cov.at[h, quarter(i)], relay_y.at[h], send_y.at[1, h], relay_y_recv.at[h], 9 + 2 * i, col).start()
            row_copy(False, h, quarter(0), 7).start()

    def relay_rows(h, start):
        def low():
            groups = pl.ds((row // 2) * QUARTER_GROUPS, QUARTER_GROUPS)
            return push(relay_y.at[h], ext.at[RIM - 1 - h, groups], relay_y_send.at[h], recv_y.at[0, h], 8, col)

        def high():
            groups = pl.ds(((row - 9) // 2) * QUARTER_GROUPS, QUARTER_GROUPS)
            return push(relay_y.at[h], ext.at[RIM + LATS + h, groups], relay_y_send.at[h], recv_y.at[1, h], 7, col)

        for cond, copy in ((low_relay, low), (high_relay, high)):
            @pl.when(cond)
            def _():
                if start:
                    push(relay_y.at[h], relay_y.at[h], relay_y_send.at[h], relay_y_recv.at[h], 7, col).wait_recv()
                    copy().start()
                else:
                    copy().wait_send()

    own_low, own_high = pl.ds(EDGE, EDGE), pl.ds(WIDTH, EDGE)
    rim_low, rim_high = pl.ds(0, EDGE), pl.ds(EDGE + WIDTH, EDGE)
    first_half, second_half = pl.ds(0, HALF_GROUPS), pl.ds(HALF_GROUPS, HALF_GROUPS)

    def col_copy(up, lat, groups):
        side = 0 if up else 1
        return push(
            half.at[lat, groups, :, own_high if up else own_low],
            half.at[lat, groups, :, rim_low if up else rim_high],
            send_x.at[side, lat], recv_x.at[side, lat], row, col + 1 if up else col - 1,
        )

    def to_relay(up, lat):
        side = 0 if up else 1
        return push(
            half.at[lat, first_half, :, own_high if up else own_low], relay_x.at[lat],
            send_x.at[side, lat], relay_x_recv.at[lat], row, col - 3 if up else col + 3,
        )

    def from_relay(up, lat):
        return push(
            relay_x.at[lat], half.at[lat, first_half, :, rim_low if up else rim_high],
            relay_x_send.at[lat], recv_x.at[0 if up else 1, lat], row, col + 4 if up else col - 4,
        )

    def send_cols(lat):
        for up, wraps, inner in (
            (True, wrap_up, (col < 15) & ~last_x),
            (False, wrap_down, (col > 0) & ~first_x),
        ):
            @pl.when(wraps)
            def _():
                to_relay(up, lat).start()
                col_copy(up, lat, second_half).start()

            @pl.when(inner)
            def _():
                col_copy(up, lat, every).start()

    def relay_cols(lat, start):
        for up, cond in ((True, relay_up), (False, relay_down)):
            @pl.when(cond)
            def _():
                if start:
                    to_relay(up, lat).wait_recv()
                    from_relay(up, lat).start()
                else:
                    from_relay(up, lat).wait_send()

    lane = lax.broadcasted_iota(jnp.int32, (8, EDGE), 0)

    def row_stage(stage, lat, start, width):
        src, shift = ((ext, RIM), (one, 2), (two, 1))[stage]
        dst, dst_shift = ((one, 2), (two, 1), (half, 0))[stage]
        scale = (THIRD, 0.5, 1.0)[stage]
        at_cols = pl.ds(start, width)
        copies = width // LON
        sub = lane[:, :width]

        def block(i):
            return src[lat + shift, i, :, at_cols]

        def up(x):
            return pltpu.roll(x, 7, 0)

        def down(x):
            return pltpu.roll(x, 1, 0)

        centre = block(0)
        start_up = up(centre)
        now_up, last_down = start_up, down(block(GROUPS - 1))
        for i in range(GROUPS):
            following = block(i + 1) if i < GROUPS - 1 else None
            next_up = up(following) if i < GROUPS - 1 else start_up
            now_down = down(centre)
            east = jnp.where(sub == 7, next_up, now_up)
            west = jnp.where(sub == 0, last_down, now_down)
            coefs = [jnp.concatenate([rows_coef[n, lat + 2, i]] * copies, axis=1) for n in range(5)]
            value = combine(
                centre, src[lat + shift + 1, i, :, at_cols], src[lat + shift - 1, i, :, at_cols], east, west, coefs
            )
            base = ext[lat + RIM, i, :, at_cols] if stage else centre
            result = base + value * scale if stage < 2 else base + value
            if stage < 2:
                dst[lat + dst_shift, i, :, at_cols] = result
            else:
                half[lat, i, :, pl.ds(start + EDGE, width)] = result
            centre, now_up, last_down = following, next_up, now_down

    def row_phase(lats, starts, width):
        for stage in range(3):
            low, count, step = lats[stage]

            def body(n, _):
                lat = low + (n // len(starts)) * step
                offset = starts[0] if len(starts) == 1 else pl.multiple_of((n % 2) * (starts[1] - starts[0]) + starts[0], LON)
                row_stage(stage, lat, offset, width)
                return 0

            lax.fori_loop(0, count * len(starts), body, 0)

    outer = (0, WIDTH - EDGE)
    load.wait()
    first = ((1, 6, 1), (2, 4, 1), (3, 2, 1))
    row_phase(first, outer, EDGE)
    send_cols(3)
    send_cols(4)
    relay_rows(0, True)
    row_phase(first, (EDGE,), WIDTH - 2 * EDGE)

    for p in range(1, 4):
        @pl.when(row > 0)
        def _():
            row_copy(True, p - 1, every, row).wait_recv()

        @pl.when(row < 15)
        def _():
            row_copy(False, p - 1, every, row).wait_recv()

        lats = tuple((s + 1 - p, 2, 5 - 2 * s + 2 * p) for s in range(3))
        row_phase(lats, outer, EDGE)
        send_cols(3 - p)
        send_cols(4 + p)
        if p < 3:
            relay_rows(p, True)
        row_phase(lats, (EDGE,), WIDTH - 2 * EDGE)
        if p > 1:
            relay_cols(5 - p, True)
            relay_cols(2 + p, True)

    load_noise.wait()

    def col_stage(centre, north, south, lat):
        east = pltpu.roll(centre, LON - 1, 2)
        west = pltpu.roll(centre, 1, 2)
        return combine(centre, north, south, east, west, [cols_coef[n, lat + 2] for n in range(5)])

    def finish(lat):
        @pl.when(col > 0)
        def _():
            col_copy(True, lat, every).wait_recv()

        @pl.when(col < 15)
        def _():
            col_copy(False, lat, every).wait_recv()

        def body(g, _):
            groups = pl.ds(g * 2, 2)
            u, v, w = {}, {}, {}
            for a in range(-3, LATS + 3):
                u[a] = half[lat, groups, :, pl.ds((a + RIM) * LON, LON)]
                b = a - 1
                if b >= -2:
                    v[b] = u[b] + THIRD * col_stage(u[b], u[b + 1], u[b - 1], b)
                b = a - 2
                if b >= -1:
                    w[b] = u[b] + 0.5 * col_stage(v[b], v[b + 1], v[b - 1], b)
                b = a - 3
                if b >= 0:
                    value = u[b] + col_stage(w[b], w[b + 1], w[b - 1], b)
                    at_cols = pl.ds(b * LON, LON)
                    out[lat, groups, :, at_cols] = out[lat, groups, :, at_cols] + value
            return 0

        lax.fori_loop(0, GROUPS // 2, body, 0)

    for q in range(4):
        finish(3 - q)
        finish(4 + q)
        if q < 2:
            relay_cols(1 - q, True)
            relay_cols(6 + q, True)

    for h in range(RIM):
        @pl.when(row < 15)
        def _():
            row_copy(True, h, every, row).wait_send()

        @pl.when(row > 0)
        def _():
            row_copy(False, h, every, row).wait_send()

        relay_rows(h, False)
    for lat in range(LATS):
        @pl.when(col < 15)
        def _():
            col_copy(True, lat, every).wait_send()

        @pl.when(col > 0)
        def _():
            col_copy(False, lat, every).wait_send()

        relay_cols(lat, False)


def shards(cov, noise, velocity_x, velocity_y, diffusion):
    shape = (LATS, GROUPS, 8, WIDTH)
    f32 = jnp.float32
    dma = pltpu.SemaphoreType.DMA
    vmem = pl.BlockSpec(memory_space=pltpu.VMEM)
    hbm = pl.BlockSpec(memory_space=pl.ANY)
    result = pl.pallas_call(
        kernel,
        out_shape=jax.ShapeDtypeStruct(shape, f32),
        in_specs=[hbm, hbm, vmem, vmem, vmem],
        out_specs=vmem,
        scratch_shapes=[
            pltpu.VMEM((LATS + 6, GROUPS, 8, WIDTH), f32),
            pltpu.VMEM((LATS + 4, GROUPS, 8, WIDTH), f32),
            pltpu.VMEM((LATS + 2, GROUPS, 8, WIDTH), f32),
            pltpu.VMEM((LATS, GROUPS, 8, WIDTH + 2 * EDGE), f32),
            pltpu.VMEM((5, LATS + 4, GROUPS, 8, LON), f32),
            pltpu.VMEM((5, LATS + 4, 8, LON), f32),
            pltpu.VMEM((LATS, HALF_GROUPS, 8, EDGE), f32),
            pltpu.VMEM((RIM, QUARTER_GROUPS, 8, WIDTH), f32),
            dma((2,)),
            dma((2, LATS)), dma((2, LATS)),
            dma((2, RIM)), dma((2, RIM)),
            dma((LATS,)), dma((LATS,)),
            dma((RIM,)), dma((RIM,)),
        ],
        compiler_params=pltpu.CompilerParams(
            collective_id=0, has_side_effects=True, vmem_limit_bytes=50 * 1024 * 1024
        ),
        name="forecast",
    )(cov.reshape(shape), noise.reshape(shape), velocity_x, velocity_y, diffusion)
    return result.reshape(WIDTH, WIDTH)


def solution(mesh):
    in_specs = (P("row", "col"), P("row", "col"), P(), P(), P())
    out_specs = P("row", "col")
    return jax.shard_map(shards, mesh=mesh, in_specs=in_specs, out_specs=out_specs, check_vma=False)
```

```python
import jax
import jax.numpy as jnp
from jax import lax
from jax.experimental import pallas as pl
from jax.experimental.pallas import tpu as pltpu
from jax.sharding import PartitionSpec as P

LATS = 8
GROUPS = 16
LON = 128
RIM = 3
WIDTH = LATS * LON
EDGE = RIM * LON
RELAYED = (0, 6, 10, 12, 12, 10, 6, 0)
QUARTER_GROUPS = GROUPS // 4
THIRD = 1.0 / 3.0


def combine(centre, north, south, east, west, coefs):
    c_east, c_west, c_north, c_south, c_centre = coefs
    return (
        (c_east * east + c_west * west)
        + (c_north * north + c_south * south)
        + c_centre * centre
    )


def coefficients(kappa, half_x, half_y):
    return (kappa - half_x, kappa + half_x, kappa - half_y, kappa + half_y, -4.0 * kappa)


def kernel(
    cov, noise, vel_x_hbm, vel_y_hbm, diffusion_hbm, out,
    vel_x, vel_y, diffusion, ext, one, two, half, rows_coef, cols_coef, relay_x, relay_y,
    load_sem, send_x, recv_x, send_y, recv_y, relay_x_recv, relay_x_send, relay_y_recv, relay_y_send,
):
    row, col = lax.axis_index("row"), lax.axis_index("col")
    pos_x, z_hi = col % 4, col // 4
    first_x, last_x = pos_x == 0, pos_x == 3
    wrap_up = last_x & (col < 15)
    wrap_down = first_x & (col > 0)
    relay_up = first_x & (z_hi < 3)
    relay_down = last_x & (z_hi > 0)
    outer_x = first_x | last_x
    low_relay = outer_x & ((row == 0) | (row == 2) | (row == 4))
    high_relay = outer_x & ((row == 11) | (row == 13) | (row == 15))

    def at(r, c):
        return {"row": r, "col": c}

    barrier = pltpu.get_barrier_semaphore()
    greeted = jnp.int32(0)
    peers = [
        (row > 0, row - 1, col), (row < 15, row + 1, col), (col > 0, row, col - 1), (col < 15, row, col + 1),
        (first_x, row, col + 3), (last_x, row, col - 3),
        (outer_x & (z_hi < 3), row, col + 4), (outer_x & (z_hi > 0), row, col - 4),
        (low_relay | high_relay, 7, col), (low_relay | high_relay, 8, col),
    ]
    for other in (0, 2, 4, 11, 13, 15):
        peers.append((outer_x & ((row == 7) | (row == 8)), other, col))
    for cond, r, c in peers:
        @pl.when(cond)
        def _(r=r, c=c):
            pl.semaphore_signal(barrier, 1, device_id=at(r, c))

        greeted = greeted + cond.astype(jnp.int32)

    fields = [
        pltpu.make_async_copy(src, dst, load_sem.at[2 + n])
        for n, (src, dst) in enumerate(((diffusion_hbm, diffusion), (vel_x_hbm, vel_x), (vel_y_hbm, vel_y)))
    ]
    for field in fields:
        field.start()
    load = pltpu.make_async_copy(cov, ext.at[RIM : RIM + LATS], load_sem.at[0])
    load.start()
    load_noise = pltpu.make_async_copy(noise, out, load_sem.at[1])
    load_noise.start()

    for field in fields:
        field.wait()

    def build(i, _):
        def at_latitude(lat):
            valid = ((lat >= 0) & (lat < 128)).astype(jnp.float32)
            lat = jnp.clip(lat, 0, 127)
            pick = pl.ds(lat, 1)
            return diffusion[pick, :] * valid, vel_x[pick, :] * (0.5 * valid), vel_y[pick, :] * (0.5 * valid)

        wide = [jnp.broadcast_to(f, (8, LON)) for f in at_latitude(col * LATS - 2 + i)]
        for n, value in enumerate(coefficients(*wide)):
            cols_coef[n, i] = value
        tall = [jnp.broadcast_to(f, (LON, LON)).T for f in at_latitude(row * LATS - 2 + i)]
        for n, value in enumerate(coefficients(*tall)):
            rows_coef[n, i] = value.reshape(GROUPS, 8, LON)
        return 0

    lax.fori_loop(0, LATS + 4, build, 0)

    @pl.when(row == 0)
    def _():
        ext[0:RIM] = jnp.zeros((RIM, GROUPS, 8, WIDTH), jnp.float32)

    @pl.when(row == 15)
    def _():
        ext[RIM + LATS :] = jnp.zeros((RIM, GROUPS, 8, WIDTH), jnp.float32)

    @pl.when(col == 0)
    def _():
        half[:, :, :, 0:EDGE] = jnp.zeros((LATS, GROUPS, 8, EDGE), jnp.float32)

    @pl.when(col == 15)
    def _():
        half[:, :, :, EDGE + WIDTH :] = jnp.zeros((LATS, GROUPS, 8, EDGE), jnp.float32)

    pl.semaphore_wait(barrier, greeted)

    def push(src, dst, send, recv, r, c):
        return pltpu.make_async_remote_copy(src, dst, send, recv, device_id=at(r, c))

    def row_copy(up, h, groups, r):
        lat, slot = (LATS - 1 - h, RIM - 1 - h) if up else (h, RIM + LATS + h)
        side = 0 if up else 1
        return push(cov.at[lat, groups], ext.at[slot, groups], send_y.at[side, h], recv_y.at[side, h], r, col)

    every = pl.ds(0, GROUPS)

    def quarter(i):
        return pl.ds(i * QUARTER_GROUPS, QUARTER_GROUPS)

    for h in range(RIM):
        @pl.when((row < 15) & ~((row == 7) & outer_x))
        def _():
            row_copy(True, h, every, row + 1).start()

        @pl.when((row > 0) & ~((row == 8) & outer_x))
        def _():
            row_copy(False, h, every, row - 1).start()

        @pl.when((row == 7) & outer_x)
        def _():
            for i in range(3):
                push(cov.at[LATS - 1 - h, quarter(i)], relay_y.at[h], send_y.at[0, h], relay_y_recv.at[h], 2 * i, col).start()
            row_copy(True, h, quarter(3), 8).start()

        @pl.when((row == 8) & outer_x)
        def _():
            for i in range(1, 4):
                push(cov.at[h, quarter(i)], relay_y.at[h], send_y.at[1, h], relay_y_recv.at[h], 9 + 2 * i, col).start()
            row_copy(False, h, quarter(0), 7).start()

    def relay_rows(h, start):
        def low():
            groups = pl.ds((row // 2) * QUARTER_GROUPS, QUARTER_GROUPS)
            return push(relay_y.at[h], ext.at[RIM - 1 - h, groups], relay_y_send.at[h], recv_y.at[0, h], 8, col)

        def high():
            groups = pl.ds(((row - 9) // 2) * QUARTER_GROUPS, QUARTER_GROUPS)
            return push(relay_y.at[h], ext.at[RIM + LATS + h, groups], relay_y_send.at[h], recv_y.at[1, h], 7, col)

        for cond, copy in ((low_relay, low), (high_relay, high)):
            @pl.when(cond)
            def _():
                if start:
                    push(relay_y.at[h], relay_y.at[h], relay_y_send.at[h], relay_y_recv.at[h], 7, col).wait_recv()
                    copy().start()
                else:
                    copy().wait_send()

    own_low, own_high = pl.ds(EDGE, EDGE), pl.ds(WIDTH, EDGE)
    rim_low, rim_high = pl.ds(0, EDGE), pl.ds(EDGE + WIDTH, EDGE)

    def relayed(lat):
        return pl.ds(0, RELAYED[lat])


    def col_copy(up, lat, groups):
        side = 0 if up else 1
        return push(
            half.at[lat, groups, :, own_high if up else own_low],
            half.at[lat, groups, :, rim_low if up else rim_high],
            send_x.at[side, lat], recv_x.at[side, lat], row, col + 1 if up else col - 1,
        )

    def to_relay(up, lat):
        side = 0 if up else 1
        return push(
            half.at[lat, relayed(lat), :, own_high if up else own_low], relay_x.at[lat, relayed(lat)],
            send_x.at[side, lat], relay_x_recv.at[lat], row, col - 3 if up else col + 3,
        )

    def from_relay(up, lat):
        return push(
            relay_x.at[lat, relayed(lat)], half.at[lat, relayed(lat), :, rim_low if up else rim_high],
            relay_x_send.at[lat], recv_x.at[0 if up else 1, lat], row, col + 4 if up else col - 4,
        )

    def send_cols(lats):
        for up, wraps in ((True, wrap_up), (False, wrap_down)):
            @pl.when(wraps)
            def _():
                for lat in lats:
                    if RELAYED[lat]:
                        to_relay(up, lat).start()

        for up, wraps in ((True, wrap_up), (False, wrap_down)):
            @pl.when(wraps)
            def _():
                for lat in lats:
                    col_copy(up, lat, pl.ds(RELAYED[lat], GROUPS - RELAYED[lat])).start()

        for up, inner in ((True, (col < 15) & ~last_x), (False, (col > 0) & ~first_x)):
            @pl.when(inner)
            def _():
                for lat in lats:
                    col_copy(up, lat, every).start()

    def relay_cols(lat, start):
        if not RELAYED[lat]:
            return
        for up, cond in ((True, relay_up), (False, relay_down)):
            @pl.when(cond)
            def _():
                if start:
                    to_relay(up, lat).wait_recv()
                    from_relay(up, lat).start()
                else:
                    from_relay(up, lat).wait_send()

    lane = lax.broadcasted_iota(jnp.int32, (8, EDGE), 0)

    def row_stage(stage, lat, start, width):
        src, shift = ((ext, RIM), (one, 2), (two, 1))[stage]
        dst, dst_shift = ((one, 2), (two, 1), (half, 0))[stage]
        scale = (THIRD, 0.5, 1.0)[stage]
        at_cols = pl.ds(start, width)
        copies = width // LON
        sub = lane[:, :width]

        def block(i):
            return src[lat + shift, i, :, at_cols]

        def up(x):
            return pltpu.roll(x, 7, 0)

        def down(x):
            return pltpu.roll(x, 1, 0)

        centre = block(0)
        start_up = up(centre)
        now_up, last_down = start_up, down(block(GROUPS - 1))
        for i in range(GROUPS):
            following = block(i + 1) if i < GROUPS - 1 else None
            next_up = up(following) if i < GROUPS - 1 else start_up
            now_down = down(centre)
            east = jnp.where(sub == 7, next_up, now_up)
            west = jnp.where(sub == 0, last_down, now_down)
            coefs = [jnp.concatenate([rows_coef[n, lat + 2, i]] * copies, axis=1) for n in range(5)]
            value = combine(
                centre, src[lat + shift + 1, i, :, at_cols], src[lat + shift - 1, i, :, at_cols], east, west, coefs
            )
            base = ext[lat + RIM, i, :, at_cols] if stage else centre
            result = base + value * scale if stage < 2 else base + value
            if stage < 2:
                dst[lat + dst_shift, i, :, at_cols] = result
            else:
                half[lat, i, :, pl.ds(start + EDGE, width)] = result
            centre, now_up, last_down = following, next_up, now_down

    def row_phase(lats, starts, width):
        for stage in range(3):
            low, count, step = lats[stage]

            def body(n, _):
                lat = low + (n // len(starts)) * step
                offset = starts[0] if len(starts) == 1 else pl.multiple_of((n % 2) * (starts[1] - starts[0]) + starts[0], LON)
                row_stage(stage, lat, offset, width)
                return 0

            lax.fori_loop(0, count * len(starts), body, 0)

    outer = (0, WIDTH - EDGE)
    load.wait()
    first = ((1, 6, 1), (2, 4, 1), (3, 2, 1))
    row_phase(first, outer, EDGE)
    send_cols((3, 4))
    relay_rows(0, True)
    row_phase(first, (EDGE,), WIDTH - 2 * EDGE)
    relay_rows(1, True)

    for p in range(1, 4):
        @pl.when(row > 0)
        def _():
            row_copy(True, p - 1, every, row).wait_recv()

        @pl.when(row < 15)
        def _():
            row_copy(False, p - 1, every, row).wait_recv()

        lats = tuple((s + 1 - p, 2, 5 - 2 * s + 2 * p) for s in range(3))
        row_phase(lats, outer, EDGE)
        send_cols((3 - p, 4 + p))
        if p == 1:
            relay_rows(2, True)
        row_phase(lats, (EDGE,), WIDTH - 2 * EDGE)
        if p == 1:
            relay_cols(3, True)
            relay_cols(4, True)
        if p == 3:
            relay_cols(2, True)
            relay_cols(5, True)

    def col_stage(stage, lat, groups, b):
        slot = pl.ds(pl.multiple_of(lat * LON, LON), LON)

        def read(level, at):
            if level == 0:
                return half[lat, groups, :, (at + RIM) * LON : (at + RIM + 1) * LON]
            return (one, two)[level - 1][at + 3 - level, groups, :, slot]

        centre = read(stage, b)
        value = combine(
            centre, read(stage, b + 1), read(stage, b - 1),
            pltpu.roll(centre, LON - 1, 2), pltpu.roll(centre, 1, 2), [cols_coef[n, b + 2] for n in range(5)],
        )
        base = read(0, b) if stage else centre
        if stage == 0:
            one[b + 2, groups, :, slot] = base + THIRD * value
        elif stage == 1:
            two[b + 1, groups, :, slot] = base + 0.5 * value
        else:
            at_cols = pl.ds(b * LON, LON)
            out[lat, groups, :, at_cols] = out[lat, groups, :, at_cols] + (base + value)

    inner = (range(1, 7), range(2, 6), range(3, 5))
    rims = ((-2, -1, 0, 7, 8, 9), (-1, 0, 1, 6, 7, 8), (0, 1, 2, 5, 6, 7))

    def col_part(low, step, parts):
        def body(n, _):
            groups = pl.ds((n % 2) * (GROUPS // 2), GROUPS // 2)
            for stage in range(3):
                for b in parts[stage]:
                    col_stage(stage, low + (n // 2) * step, groups, b)
            return 0

        lax.fori_loop(0, 4, body, 0)

    def arrive(lat):
        @pl.when(col > 0)
        def _():
            col_copy(True, lat, every).wait_recv()

        @pl.when(col < 15)
        def _():
            col_copy(False, lat, every).wait_recv()

    load_noise.wait()
    for q in range(4):
        col_part(3 - q, 2 * q + 1, inner)
        if q == 1:
            relay_cols(1, True)
            relay_cols(6, True)
            relay_cols(0, True)
            relay_cols(7, True)
    for q in range(4):
        arrive(3 - q)
        arrive(4 + q)
        col_part(3 - q, 2 * q + 1, rims)

    for h in range(RIM):
        @pl.when(row < 15)
        def _():
            row_copy(True, h, every, row).wait_send()

        @pl.when(row > 0)
        def _():
            row_copy(False, h, every, row).wait_send()

        relay_rows(h, False)
    for lat in range(LATS):
        @pl.when(col < 15)
        def _():
            col_copy(True, lat, every).wait_send()

        @pl.when(col > 0)
        def _():
            col_copy(False, lat, every).wait_send()

        relay_cols(lat, False)


def shards(cov, noise, velocity_x, velocity_y, diffusion):
    shape = (LATS, GROUPS, 8, WIDTH)
    f32 = jnp.float32
    dma = pltpu.SemaphoreType.DMA
    vmem = pl.BlockSpec(memory_space=pltpu.VMEM)
    hbm = pl.BlockSpec(memory_space=pltpu.HBM)
    result = pl.pallas_call(
        kernel,
        out_shape=jax.ShapeDtypeStruct(shape, f32),
        in_specs=[hbm] * 5,
        out_specs=vmem,
        scratch_shapes=[
            pltpu.VMEM((128, LON), f32), pltpu.VMEM((128, LON), f32), pltpu.VMEM((128, LON), f32),
            pltpu.VMEM((LATS + 6, GROUPS, 8, WIDTH), f32),
            pltpu.VMEM((LATS + 4, GROUPS, 8, WIDTH), f32),
            pltpu.VMEM((LATS + 2, GROUPS, 8, WIDTH), f32),
            pltpu.VMEM((LATS, GROUPS, 8, WIDTH + 2 * EDGE), f32),
            pltpu.VMEM((5, LATS + 4, GROUPS, 8, LON), f32),
            pltpu.VMEM((5, LATS + 4, 8, LON), f32),
            pltpu.VMEM((LATS, max(RELAYED), 8, EDGE), f32),
            pltpu.VMEM((RIM, QUARTER_GROUPS, 8, WIDTH), f32),
            dma((5,)),
            dma((2, LATS)), dma((2, LATS)),
            dma((2, RIM)), dma((2, RIM)),
            dma((LATS,)), dma((LATS,)),
            dma((RIM,)), dma((RIM,)),
        ],
        compiler_params=pltpu.CompilerParams(
            collective_id=0, has_side_effects=True, vmem_limit_bytes=48 * 1024 * 1024
        ),
        name="forecast",
    )(cov.reshape(shape), noise.reshape(shape), velocity_x, velocity_y, diffusion)
    return result.reshape(WIDTH, WIDTH)


def solution(mesh):
    in_specs = (P("row", "col"), P("row", "col"), P(), P(), P())
    out_specs = P("row", "col")
    return jax.shard_map(shards, mesh=mesh, in_specs=in_specs, out_specs=out_specs, check_vma=False)
```

```python
import jax
import jax.numpy as jnp
from jax import lax
from jax.experimental import pallas as pl
from jax.experimental.pallas import tpu as pltpu
from jax.sharding import PartitionSpec as P

LATS = 8
GROUPS = 16
LON = 128
RIM = 3
WIDTH = LATS * LON
EDGE = RIM * LON
RELAYED = (0, 6, 10, 12, 12, 10, 6, 0)
QUARTER_GROUPS = GROUPS // 4
THIRD = 1.0 / 3.0


def combine(centre, north, south, east, west, coefs):
    c_east, c_west, c_north, c_south, c_centre = coefs
    return (
        (c_east * east + c_west * west)
        + (c_north * north + c_south * south)
        + c_centre * centre
    )


def coefficients(kappa, half_x, half_y):
    return (kappa - half_x, kappa + half_x, kappa - half_y, kappa + half_y, -4.0 * kappa)


def kernel(
    cov, noise, fields, out,
    ext, one, two, half, rows_coef, cols_coef, relay_x, relay_y,
    load_sem, send_x, recv_x, send_y, recv_y, relay_x_recv, relay_x_send, relay_y_recv, relay_y_send,
):
    row, col = lax.axis_index("row"), lax.axis_index("col")
    pos_x, z_hi = col % 4, col // 4
    first_x, last_x = pos_x == 0, pos_x == 3
    wrap_up = last_x & (col < 15)
    wrap_down = first_x & (col > 0)
    relay_up = first_x & (z_hi < 3)
    relay_down = last_x & (z_hi > 0)
    outer_x = first_x | last_x
    low_relay = outer_x & ((row == 0) | (row == 2) | (row == 4))
    high_relay = outer_x & ((row == 11) | (row == 13) | (row == 15))

    def at(r, c):
        return {"row": r, "col": c}

    barrier = pltpu.get_barrier_semaphore()
    greeted = jnp.int32(0)
    peers = [
        (row > 0, row - 1, col), (row < 15, row + 1, col), (col > 0, row, col - 1), (col < 15, row, col + 1),
        (first_x, row, col + 3), (last_x, row, col - 3),
        (outer_x & (z_hi < 3), row, col + 4), (outer_x & (z_hi > 0), row, col - 4),
        (low_relay | high_relay, 7, col), (low_relay | high_relay, 8, col),
    ]
    for other in (0, 2, 4, 11, 13, 15):
        peers.append((outer_x & ((row == 7) | (row == 8)), other, col))
    for cond, r, c in peers:
        @pl.when(cond)
        def _(r=r, c=c):
            pl.semaphore_signal(barrier, 1, device_id=at(r, c))

        greeted = greeted + cond.astype(jnp.int32)

    load = pltpu.make_async_copy(cov, ext.at[RIM : RIM + LATS], load_sem.at[0])
    load.start()
    load_noise = pltpu.make_async_copy(noise, out, load_sem.at[1])
    load_noise.start()

    def build(i, _):
        def at_latitude(lat):
            valid = ((lat >= 0) & (lat < 128)).astype(jnp.float32)
            lat = jnp.clip(lat, 0, 127)
            pick = pl.ds(lat, 1)
            kappa, vel_x, vel_y = (fields[n, pick, :] for n in range(3))
            return kappa * valid, vel_x * (0.5 * valid), vel_y * (0.5 * valid)

        wide = [jnp.broadcast_to(f, (8, LON)) for f in at_latitude(col * LATS - 2 + i)]
        for n, value in enumerate(coefficients(*wide)):
            cols_coef[n, i] = value
        tall = [jnp.broadcast_to(f, (LON, LON)).T for f in at_latitude(row * LATS - 2 + i)]
        for n, value in enumerate(coefficients(*tall)):
            rows_coef[n, i] = value.reshape(GROUPS, 8, LON)
        return 0

    lax.fori_loop(0, LATS + 4, build, 0)

    @pl.when(row == 0)
    def _():
        ext[0:RIM] = jnp.zeros((RIM, GROUPS, 8, WIDTH), jnp.float32)

    @pl.when(row == 15)
    def _():
        ext[RIM + LATS :] = jnp.zeros((RIM, GROUPS, 8, WIDTH), jnp.float32)

    @pl.when(col == 0)
    def _():
        half[:, :, :, 0:EDGE] = jnp.zeros((LATS, GROUPS, 8, EDGE), jnp.float32)

    @pl.when(col == 15)
    def _():
        half[:, :, :, EDGE + WIDTH :] = jnp.zeros((LATS, GROUPS, 8, EDGE), jnp.float32)

    pl.semaphore_wait(barrier, greeted)

    def push(src, dst, send, recv, r, c):
        return pltpu.make_async_remote_copy(src, dst, send, recv, device_id=at(r, c))

    def row_copy(up, h, groups, r):
        lat, slot = (LATS - 1 - h, RIM - 1 - h) if up else (h, RIM + LATS + h)
        side = 0 if up else 1
        return push(cov.at[lat, groups], ext.at[slot, groups], send_y.at[side, h], recv_y.at[side, h], r, col)

    every = pl.ds(0, GROUPS)

    def quarter(i):
        return pl.ds(i * QUARTER_GROUPS, QUARTER_GROUPS)

    for h in range(RIM):
        @pl.when((row < 15) & ~((row == 7) & outer_x))
        def _():
            row_copy(True, h, every, row + 1).start()

        @pl.when((row > 0) & ~((row == 8) & outer_x))
        def _():
            row_copy(False, h, every, row - 1).start()

        @pl.when((row == 7) & outer_x)
        def _():
            for i in range(3):
                push(cov.at[LATS - 1 - h, quarter(i)], relay_y.at[h], send_y.at[0, h], relay_y_recv.at[h], 2 * i, col).start()
            row_copy(True, h, quarter(3), 8).start()

        @pl.when((row == 8) & outer_x)
        def _():
            for i in range(1, 4):
                push(cov.at[h, quarter(i)], relay_y.at[h], send_y.at[1, h], relay_y_recv.at[h], 9 + 2 * i, col).start()
            row_copy(False, h, quarter(0), 7).start()

    def relay_rows(h, start):
        def low():
            groups = pl.ds((row // 2) * QUARTER_GROUPS, QUARTER_GROUPS)
            return push(relay_y.at[h], ext.at[RIM - 1 - h, groups], relay_y_send.at[h], recv_y.at[0, h], 8, col)

        def high():
            groups = pl.ds(((row - 9) // 2) * QUARTER_GROUPS, QUARTER_GROUPS)
            return push(relay_y.at[h], ext.at[RIM + LATS + h, groups], relay_y_send.at[h], recv_y.at[1, h], 7, col)

        for cond, copy in ((low_relay, low), (high_relay, high)):
            @pl.when(cond)
            def _():
                if start:
                    push(relay_y.at[h], relay_y.at[h], relay_y_send.at[h], relay_y_recv.at[h], 7, col).wait_recv()
                    copy().start()
                else:
                    copy().wait_send()

    own_low, own_high = pl.ds(EDGE, EDGE), pl.ds(WIDTH, EDGE)
    rim_low, rim_high = pl.ds(0, EDGE), pl.ds(EDGE + WIDTH, EDGE)

    def relayed(lat):
        return pl.ds(0, RELAYED[lat])


    def col_copy(up, lat, groups):
        side = 0 if up else 1
        return push(
            half.at[lat, groups, :, own_high if up else own_low],
            half.at[lat, groups, :, rim_low if up else rim_high],
            send_x.at[side, lat], recv_x.at[side, lat], row, col + 1 if up else col - 1,
        )

    def to_relay(up, lat):
        side = 0 if up else 1
        return push(
            half.at[lat, relayed(lat), :, own_high if up else own_low], relay_x.at[lat, relayed(lat)],
            send_x.at[side, lat], relay_x_recv.at[lat], row, col - 3 if up else col + 3,
        )

    def from_relay(up, lat):
        return push(
            relay_x.at[lat, relayed(lat)], half.at[lat, relayed(lat), :, rim_low if up else rim_high],
            relay_x_send.at[lat], recv_x.at[0 if up else 1, lat], row, col + 4 if up else col - 4,
        )

    def send_cols(lats):
        for up, wraps in ((True, wrap_up), (False, wrap_down)):
            @pl.when(wraps)
            def _():
                for lat in lats:
                    if RELAYED[lat]:
                        to_relay(up, lat).start()

        for up, wraps in ((True, wrap_up), (False, wrap_down)):
            @pl.when(wraps)
            def _():
                for lat in lats:
                    col_copy(up, lat, pl.ds(RELAYED[lat], GROUPS - RELAYED[lat])).start()

        for up, inner in ((True, (col < 15) & ~last_x), (False, (col > 0) & ~first_x)):
            @pl.when(inner)
            def _():
                for lat in lats:
                    col_copy(up, lat, every).start()

    def relay_cols(lat, start):
        if not RELAYED[lat]:
            return
        for up, cond in ((True, relay_up), (False, relay_down)):
            @pl.when(cond)
            def _():
                if start:
                    to_relay(up, lat).wait_recv()
                    from_relay(up, lat).start()
                else:
                    from_relay(up, lat).wait_send()

    lane = lax.broadcasted_iota(jnp.int32, (8, EDGE), 0)

    def row_stage(stage, lat, start, width):
        src, shift = ((ext, RIM), (one, 2), (two, 1))[stage]
        dst, dst_shift = ((one, 2), (two, 1), (half, 0))[stage]
        scale = (THIRD, 0.5, 1.0)[stage]
        at_cols = pl.ds(start, width)
        copies = width // LON
        sub = lane[:, :width]

        def block(i):
            return src[lat + shift, i, :, at_cols]

        def up(x):
            return pltpu.roll(x, 7, 0)

        def down(x):
            return pltpu.roll(x, 1, 0)

        centre = block(0)
        start_up = up(centre)
        now_up, last_down = start_up, down(block(GROUPS - 1))
        for i in range(GROUPS):
            following = block(i + 1) if i < GROUPS - 1 else None
            next_up = up(following) if i < GROUPS - 1 else start_up
            now_down = down(centre)
            east = jnp.where(sub == 7, next_up, now_up)
            west = jnp.where(sub == 0, last_down, now_down)
            coefs = [jnp.concatenate([rows_coef[n, lat + 2, i]] * copies, axis=1) for n in range(5)]
            value = combine(
                centre, src[lat + shift + 1, i, :, at_cols], src[lat + shift - 1, i, :, at_cols], east, west, coefs
            )
            base = ext[lat + RIM, i, :, at_cols] if stage else centre
            result = base + value * scale if stage < 2 else base + value
            if stage < 2:
                dst[lat + dst_shift, i, :, at_cols] = result
            else:
                half[lat, i, :, pl.ds(start + EDGE, width)] = result
            centre, now_up, last_down = following, next_up, now_down

    def row_phase(lats, starts, width):
        for stage in range(3):
            low, count, step = lats[stage]

            def body(n, _):
                lat = low + (n // len(starts)) * step
                offset = starts[0] if len(starts) == 1 else pl.multiple_of((n % 2) * (starts[1] - starts[0]) + starts[0], LON)
                row_stage(stage, lat, offset, width)
                return 0

            lax.fori_loop(0, count * len(starts), body, 0)

    outer = (0, WIDTH - EDGE)
    load.wait()
    first = ((1, 6, 1), (2, 4, 1), (3, 2, 1))
    row_phase(first, outer, EDGE)
    send_cols((3, 4))
    relay_rows(0, True)
    row_phase(first, (EDGE,), WIDTH - 2 * EDGE)
    relay_rows(1, True)

    for p in range(1, 4):
        @pl.when(row > 0)
        def _():
            row_copy(True, p - 1, every, row).wait_recv()

        @pl.when(row < 15)
        def _():
            row_copy(False, p - 1, every, row).wait_recv()

        lats = tuple((s + 1 - p, 2, 5 - 2 * s + 2 * p) for s in range(3))
        row_phase(lats, outer, EDGE)
        send_cols((3 - p, 4 + p))
        if p == 1:
            relay_rows(2, True)
        row_phase(lats, (EDGE,), WIDTH - 2 * EDGE)
        if p == 1:
            relay_cols(3, True)
            relay_cols(4, True)
        if p == 3:
            relay_cols(2, True)
            relay_cols(5, True)

    def col_stage(stage, lat, groups, b):
        slot = pl.ds(pl.multiple_of(lat * LON, LON), LON)

        def read(level, at):
            if level == 0:
                return half[lat, groups, :, (at + RIM) * LON : (at + RIM + 1) * LON]
            return (one, two)[level - 1][at + 3 - level, groups, :, slot]

        centre = read(stage, b)
        value = combine(
            centre, read(stage, b + 1), read(stage, b - 1),
            pltpu.roll(centre, LON - 1, 2), pltpu.roll(centre, 1, 2), [cols_coef[n, b + 2] for n in range(5)],
        )
        base = read(0, b) if stage else centre
        if stage == 0:
            one[b + 2, groups, :, slot] = base + THIRD * value
        elif stage == 1:
            two[b + 1, groups, :, slot] = base + 0.5 * value
        else:
            at_cols = pl.ds(b * LON, LON)
            out[lat, groups, :, at_cols] = out[lat, groups, :, at_cols] + (base + value)

    inner = (range(1, 7), range(2, 6), range(3, 5))
    rims = ((-2, -1, 0, 7, 8, 9), (-1, 0, 1, 6, 7, 8), (0, 1, 2, 5, 6, 7))

    def col_part(low, step, parts, count=4):
        def body(n, _):
            groups = pl.ds((n % 2) * (GROUPS // 2), GROUPS // 2)
            for stage in range(3):
                for b in parts[stage]:
                    col_stage(stage, low + (n // 2) * step, groups, b)
            return 0

        lax.fori_loop(0, count, body, 0)

    def arrive(lat):
        @pl.when(col > 0)
        def _():
            col_copy(True, lat, every).wait_recv()

        @pl.when(col < 15)
        def _():
            col_copy(False, lat, every).wait_recv()

    load_noise.wait()
    for q in range(4):
        col_part(3 - q, 2 * q + 1, inner)
        if q == 0:
            relay_cols(1, True)
            relay_cols(6, True)
            relay_cols(0, True)
            relay_cols(7, True)
    for q in range(4):
        for lat in (3 - q, 4 + q):
            arrive(lat)
            col_part(lat, 0, rims, 2)

    for h in range(RIM):
        @pl.when(row < 15)
        def _():
            row_copy(True, h, every, row).wait_send()

        @pl.when(row > 0)
        def _():
            row_copy(False, h, every, row).wait_send()

        relay_rows(h, False)
    for lat in range(LATS):
        @pl.when(col < 15)
        def _():
            col_copy(True, lat, every).wait_send()

        @pl.when(col > 0)
        def _():
            col_copy(False, lat, every).wait_send()

        relay_cols(lat, False)


def shards(cov, noise, velocity_x, velocity_y, diffusion):
    shape = (LATS, GROUPS, 8, WIDTH)
    f32 = jnp.float32
    dma = pltpu.SemaphoreType.DMA
    vmem = pl.BlockSpec(memory_space=pltpu.VMEM)
    hbm = pl.BlockSpec(memory_space=pltpu.HBM)
    result = pl.pallas_call(
        kernel,
        out_shape=jax.ShapeDtypeStruct(shape, f32),
        in_specs=[hbm, hbm, vmem],
        out_specs=vmem,
        scratch_shapes=[
            pltpu.VMEM((LATS + 6, GROUPS, 8, WIDTH), f32),
            pltpu.VMEM((LATS + 4, GROUPS, 8, WIDTH), f32),
            pltpu.VMEM((LATS + 2, GROUPS, 8, WIDTH), f32),
            pltpu.VMEM((LATS, GROUPS, 8, WIDTH + 2 * EDGE), f32),
            pltpu.VMEM((5, LATS + 4, GROUPS, 8, LON), f32),
            pltpu.VMEM((5, LATS + 4, 8, LON), f32),
            pltpu.VMEM((LATS, max(RELAYED), 8, EDGE), f32),
            pltpu.VMEM((RIM, QUARTER_GROUPS, 8, WIDTH), f32),
            dma((2,)),
            dma((2, LATS)), dma((2, LATS)),
            dma((2, RIM)), dma((2, RIM)),
            dma((LATS,)), dma((LATS,)),
            dma((RIM,)), dma((RIM,)),
        ],
        compiler_params=pltpu.CompilerParams(
            collective_id=0, has_side_effects=True, vmem_limit_bytes=48 * 1024 * 1024
        ),
        name="forecast",
    )(cov.reshape(shape), noise.reshape(shape), jnp.stack([diffusion, velocity_x, velocity_y]))
    return result.reshape(WIDTH, WIDTH)


def solution(mesh):
    in_specs = (P("row", "col"), P("row", "col"), P(), P(), P())
    out_specs = P("row", "col")
    return jax.shard_map(shards, mesh=mesh, in_specs=in_specs, out_specs=out_specs, check_vma=False)
```

```python
import jax
import jax.numpy as jnp
from jax import lax
from jax.experimental import pallas as pl
from jax.experimental.pallas import tpu as pltpu
from jax.sharding import PartitionSpec as P

LATS = 8
GROUPS = 16
LON = 128
RIM = 3
WIDTH = LATS * LON
EDGE = RIM * LON
RELAYED = (0, 6, 10, 12, 12, 10, 6, 0)
QUARTER_GROUPS = GROUPS // 4
THIRD = 1.0 / 3.0


def combine(centre, north, south, east, west, coefs):
    c_east, c_west, c_north, c_south, c_centre = coefs
    return (
        (c_east * east + c_west * west)
        + (c_north * north + c_south * south)
        + c_centre * centre
    )


def coefficients(kappa, half_x, half_y):
    return (kappa - half_x, kappa + half_x, kappa - half_y, kappa + half_y, -4.0 * kappa)


def kernel(
    cov, noise, fields, out,
    ext, one, two, half, rows_coef, cols_coef, relay_x, relay_y,
    load_sem, send_x, recv_x, send_y, recv_y, relay_x_recv, relay_x_send, relay_y_recv, relay_y_send,
):
    row, col = lax.axis_index("row"), lax.axis_index("col")
    pos_x, z_hi = col % 4, col // 4
    first_x, last_x = pos_x == 0, pos_x == 3
    wrap_up = last_x & (col < 15)
    wrap_down = first_x & (col > 0)
    relay_up = first_x & (z_hi < 3)
    relay_down = last_x & (z_hi > 0)
    outer_x = first_x | last_x
    low_relay = outer_x & ((row == 0) | (row == 2) | (row == 4))
    high_relay = outer_x & ((row == 11) | (row == 13) | (row == 15))

    def at(r, c):
        return {"row": r, "col": c}

    barrier = pltpu.get_barrier_semaphore()
    greeted = jnp.int32(0)
    peers = [
        (row > 0, row - 1, col), (row < 15, row + 1, col), (col > 0, row, col - 1), (col < 15, row, col + 1),
        (first_x, row, col + 3), (last_x, row, col - 3),
        (outer_x & (z_hi < 3), row, col + 4), (outer_x & (z_hi > 0), row, col - 4),
        (low_relay | high_relay, 7, col), (low_relay | high_relay, 8, col),
    ]
    for other in (0, 2, 4, 11, 13, 15):
        peers.append((outer_x & ((row == 7) | (row == 8)), other, col))
    for cond, r, c in peers:
        @pl.when(cond)
        def _(r=r, c=c):
            pl.semaphore_signal(barrier, 1, device_id=at(r, c))

        greeted = greeted + cond.astype(jnp.int32)

    load = pltpu.make_async_copy(cov, ext.at[RIM : RIM + LATS], load_sem.at[0])
    load.start()
    load_noise = pltpu.make_async_copy(noise, out, load_sem.at[1])
    load_noise.start()

    def build(i, _):
        def at_latitude(lat):
            valid = ((lat >= 0) & (lat < 128)).astype(jnp.float32)
            lat = jnp.clip(lat, 0, 127)
            pick = pl.ds(lat, 1)
            kappa, vel_x, vel_y = (fields[n, pick, :] for n in range(3))
            return kappa * valid, vel_x * (0.5 * valid), vel_y * (0.5 * valid)

        wide = [jnp.broadcast_to(f, (8, LON)) for f in at_latitude(col * LATS - 2 + i)]
        for n, value in enumerate(coefficients(*wide)):
            cols_coef[n, i] = value
        tall = [jnp.broadcast_to(f, (LON, LON)).T for f in at_latitude(row * LATS - 2 + i)]
        for n, value in enumerate(coefficients(*tall)):
            rows_coef[n, i] = value.reshape(GROUPS, 8, LON)
        return 0

    lax.fori_loop(0, LATS + 4, build, 0)

    @pl.when(row == 0)
    def _():
        ext[0:RIM] = jnp.zeros((RIM, GROUPS, 8, WIDTH), jnp.float32)

    @pl.when(row == 15)
    def _():
        ext[RIM + LATS :] = jnp.zeros((RIM, GROUPS, 8, WIDTH), jnp.float32)

    @pl.when(col == 0)
    def _():
        half[:, :, :, 0:EDGE] = jnp.zeros((LATS, GROUPS, 8, EDGE), jnp.float32)

    @pl.when(col == 15)
    def _():
        half[:, :, :, EDGE + WIDTH :] = jnp.zeros((LATS, GROUPS, 8, EDGE), jnp.float32)

    pl.semaphore_wait(barrier, greeted)

    def push(src, dst, send, recv, r, c):
        return pltpu.make_async_remote_copy(src, dst, send, recv, device_id=at(r, c))

    def row_copy(up, h, groups, r):
        lat, slot = (LATS - 1 - h, RIM - 1 - h) if up else (h, RIM + LATS + h)
        side = 0 if up else 1
        return push(cov.at[lat, groups], ext.at[slot, groups], send_y.at[side, h], recv_y.at[side, h], r, col)

    every = pl.ds(0, GROUPS)

    def quarter(i):
        return pl.ds(i * QUARTER_GROUPS, QUARTER_GROUPS)

    def send_rows(h):
        @pl.when((row < 15) & ~((row == 7) & outer_x))
        def _():
            row_copy(True, h, every, row + 1).start()

        @pl.when((row > 0) & ~((row == 8) & outer_x))
        def _():
            row_copy(False, h, every, row - 1).start()

        @pl.when((row == 7) & outer_x)
        def _():
            for i in range(3):
                push(cov.at[LATS - 1 - h, quarter(i)], relay_y.at[h], send_y.at[0, h], relay_y_recv.at[h], 2 * i, col).start()
            row_copy(True, h, quarter(3), 8).start()

        @pl.when((row == 8) & outer_x)
        def _():
            for i in range(1, 4):
                push(cov.at[h, quarter(i)], relay_y.at[h], send_y.at[1, h], relay_y_recv.at[h], 9 + 2 * i, col).start()
            row_copy(False, h, quarter(0), 7).start()

    send_rows(0)

    def relay_rows(h, start):
        def low():
            groups = pl.ds((row // 2) * QUARTER_GROUPS, QUARTER_GROUPS)
            return push(relay_y.at[h], ext.at[RIM - 1 - h, groups], relay_y_send.at[h], recv_y.at[0, h], 8, col)

        def high():
            groups = pl.ds(((row - 9) // 2) * QUARTER_GROUPS, QUARTER_GROUPS)
            return push(relay_y.at[h], ext.at[RIM + LATS + h, groups], relay_y_send.at[h], recv_y.at[1, h], 7, col)

        for cond, copy in ((low_relay, low), (high_relay, high)):
            @pl.when(cond)
            def _():
                if start:
                    push(relay_y.at[h], relay_y.at[h], relay_y_send.at[h], relay_y_recv.at[h], 7, col).wait_recv()
                    copy().start()
                else:
                    copy().wait_send()

    own_low, own_high = pl.ds(EDGE, EDGE), pl.ds(WIDTH, EDGE)
    rim_low, rim_high = pl.ds(0, EDGE), pl.ds(EDGE + WIDTH, EDGE)

    def relayed(lat):
        return pl.ds(0, RELAYED[lat])


    def col_copy(up, lat, groups):
        side = 0 if up else 1
        return push(
            half.at[lat, groups, :, own_high if up else own_low],
            half.at[lat, groups, :, rim_low if up else rim_high],
            send_x.at[side, lat], recv_x.at[side, lat], row, col + 1 if up else col - 1,
        )

    def to_relay(up, lat):
        side = 0 if up else 1
        return push(
            half.at[lat, relayed(lat), :, own_high if up else own_low], relay_x.at[lat, relayed(lat)],
            send_x.at[side, lat], relay_x_recv.at[lat], row, col - 3 if up else col + 3,
        )

    def from_relay(up, lat):
        return push(
            relay_x.at[lat, relayed(lat)], half.at[lat, relayed(lat), :, rim_low if up else rim_high],
            relay_x_send.at[lat], recv_x.at[0 if up else 1, lat], row, col + 4 if up else col - 4,
        )

    def send_cols(lats):
        for up, wraps in ((True, wrap_up), (False, wrap_down)):
            @pl.when(wraps)
            def _():
                for lat in lats:
                    if RELAYED[lat]:
                        to_relay(up, lat).start()

        for up, wraps in ((True, wrap_up), (False, wrap_down)):
            @pl.when(wraps)
            def _():
                for lat in lats:
                    col_copy(up, lat, pl.ds(RELAYED[lat], GROUPS - RELAYED[lat])).start()

        for up, inner in ((True, (col < 15) & ~last_x), (False, (col > 0) & ~first_x)):
            @pl.when(inner)
            def _():
                for lat in lats:
                    col_copy(up, lat, every).start()

    def relay_cols(lat, start):
        if not RELAYED[lat]:
            return
        for up, cond in ((True, relay_up), (False, relay_down)):
            @pl.when(cond)
            def _():
                if start:
                    to_relay(up, lat).wait_recv()
                    from_relay(up, lat).start()
                else:
                    from_relay(up, lat).wait_send()

    lane = lax.broadcasted_iota(jnp.int32, (8, EDGE), 0)

    def row_stage(stage, lat, start, width):
        src, shift = ((ext, RIM), (one, 2), (two, 1))[stage]
        dst, dst_shift = ((one, 2), (two, 1), (half, 0))[stage]
        scale = (THIRD, 0.5, 1.0)[stage]
        at_cols = pl.ds(start, width)
        copies = width // LON
        sub = lane[:, :width]

        def block(i):
            return src[lat + shift, i, :, at_cols]

        def up(x):
            return pltpu.roll(x, 7, 0)

        def down(x):
            return pltpu.roll(x, 1, 0)

        centre = block(0)
        start_up = up(centre)
        now_up, last_down = start_up, down(block(GROUPS - 1))
        for i in range(GROUPS):
            following = block(i + 1) if i < GROUPS - 1 else None
            next_up = up(following) if i < GROUPS - 1 else start_up
            now_down = down(centre)
            east = jnp.where(sub == 7, next_up, now_up)
            west = jnp.where(sub == 0, last_down, now_down)
            coefs = [jnp.concatenate([rows_coef[n, lat + 2, i]] * copies, axis=1) for n in range(5)]
            value = combine(
                centre, src[lat + shift + 1, i, :, at_cols], src[lat + shift - 1, i, :, at_cols], east, west, coefs
            )
            base = ext[lat + RIM, i, :, at_cols] if stage else centre
            result = base + value * scale if stage < 2 else base + value
            if stage < 2:
                dst[lat + dst_shift, i, :, at_cols] = result
            else:
                half[lat, i, :, pl.ds(start + EDGE, width)] = result
            centre, now_up, last_down = following, next_up, now_down

    def row_phase(lats, starts, width):
        for stage in range(3):
            low, count, step = lats[stage]

            def body(n, _):
                lat = low + (n // len(starts)) * step
                offset = starts[0] if len(starts) == 1 else pl.multiple_of((n % 2) * (starts[1] - starts[0]) + starts[0], LON)
                row_stage(stage, lat, offset, width)
                return 0

            lax.fori_loop(0, count * len(starts), body, 0)

    outer = (0, WIDTH - EDGE)
    load.wait()
    first = ((1, 6, 1), (2, 4, 1), (3, 2, 1))
    row_phase(first, outer, EDGE)
    send_cols((3, 4))
    send_rows(1)
    send_rows(2)
    relay_rows(0, True)
    row_phase(first, (EDGE,), WIDTH - 2 * EDGE)
    relay_rows(1, True)

    for p in range(1, 4):
        @pl.when(row > 0)
        def _():
            row_copy(True, p - 1, every, row).wait_recv()

        @pl.when(row < 15)
        def _():
            row_copy(False, p - 1, every, row).wait_recv()

        lats = tuple((s + 1 - p, 2, 5 - 2 * s + 2 * p) for s in range(3))
        row_phase(lats, outer, EDGE)
        send_cols((3 - p, 4 + p))
        if p == 1:
            relay_rows(2, True)
        row_phase(lats, (EDGE,), WIDTH - 2 * EDGE)
        if p == 1:
            relay_cols(3, True)
            relay_cols(4, True)
        if p == 3:
            relay_cols(2, True)
            relay_cols(5, True)

    def col_stage(stage, lat, groups, b):
        slot = pl.ds(pl.multiple_of(lat * LON, LON), LON)

        def read(level, at):
            if level == 0:
                return half[lat, groups, :, (at + RIM) * LON : (at + RIM + 1) * LON]
            return (one, two)[level - 1][at + 3 - level, groups, :, slot]

        centre = read(stage, b)
        value = combine(
            centre, read(stage, b + 1), read(stage, b - 1),
            pltpu.roll(centre, LON - 1, 2), pltpu.roll(centre, 1, 2), [cols_coef[n, b + 2] for n in range(5)],
        )
        base = read(0, b) if stage else centre
        if stage == 0:
            one[b + 2, groups, :, slot] = base + THIRD * value
        elif stage == 1:
            two[b + 1, groups, :, slot] = base + 0.5 * value
        else:
            at_cols = pl.ds(b * LON, LON)
            out[lat, groups, :, at_cols] = out[lat, groups, :, at_cols] + (base + value)

    inner = (range(1, 7), range(2, 6), range(3, 5))
    rims = ((-2, -1, 0, 7, 8, 9), (-1, 0, 1, 6, 7, 8), (0, 1, 2, 5, 6, 7))

    def col_part(low, step, parts, count=4):
        def body(n, _):
            groups = pl.ds((n % 2) * (GROUPS // 2), GROUPS // 2)
            for stage in range(3):
                for b in parts[stage]:
                    col_stage(stage, low + (n // 2) * step, groups, b)
            return 0

        lax.fori_loop(0, count, body, 0)

    def arrive(lat):
        @pl.when(col > 0)
        def _():
            col_copy(True, lat, every).wait_recv()

        @pl.when(col < 15)
        def _():
            col_copy(False, lat, every).wait_recv()

    load_noise.wait()
    for q in range(4):
        col_part(3 - q, 2 * q + 1, inner)
        if q == 0:
            relay_cols(1, True)
            relay_cols(6, True)
            relay_cols(0, True)
            relay_cols(7, True)
    for q in range(4):
        for lat in (3 - q, 4 + q):
            arrive(lat)
            col_part(lat, 0, rims, 2)

    for h in range(RIM):
        @pl.when(row < 15)
        def _():
            row_copy(True, h, every, row).wait_send()

        @pl.when(row > 0)
        def _():
            row_copy(False, h, every, row).wait_send()

        relay_rows(h, False)
    for lat in range(LATS):
        @pl.when(col < 15)
        def _():
            col_copy(True, lat, every).wait_send()

        @pl.when(col > 0)
        def _():
            col_copy(False, lat, every).wait_send()

        relay_cols(lat, False)


def shards(cov, noise, velocity_x, velocity_y, diffusion):
    shape = (LATS, GROUPS, 8, WIDTH)
    f32 = jnp.float32
    dma = pltpu.SemaphoreType.DMA
    vmem = pl.BlockSpec(memory_space=pltpu.VMEM)
    hbm = pl.BlockSpec(memory_space=pltpu.HBM)
    result = pl.pallas_call(
        kernel,
        out_shape=jax.ShapeDtypeStruct(shape, f32),
        in_specs=[hbm, hbm, vmem],
        out_specs=vmem,
        scratch_shapes=[
            pltpu.VMEM((LATS + 6, GROUPS, 8, WIDTH), f32),
            pltpu.VMEM((LATS + 4, GROUPS, 8, WIDTH), f32),
            pltpu.VMEM((LATS + 2, GROUPS, 8, WIDTH), f32),
            pltpu.VMEM((LATS, GROUPS, 8, WIDTH + 2 * EDGE), f32),
            pltpu.VMEM((5, LATS + 4, GROUPS, 8, LON), f32),
            pltpu.VMEM((5, LATS + 4, 8, LON), f32),
            pltpu.VMEM((LATS, max(RELAYED), 8, EDGE), f32),
            pltpu.VMEM((RIM, QUARTER_GROUPS, 8, WIDTH), f32),
            dma((2,)),
            dma((2, LATS)), dma((2, LATS)),
            dma((2, RIM)), dma((2, RIM)),
            dma((LATS,)), dma((LATS,)),
            dma((RIM,)), dma((RIM,)),
        ],
        compiler_params=pltpu.CompilerParams(
            collective_id=0, has_side_effects=True, vmem_limit_bytes=48 * 1024 * 1024
        ),
        name="forecast",
    )(cov.reshape(shape), noise.reshape(shape), jnp.stack([diffusion, velocity_x, velocity_y]))
    return result.reshape(WIDTH, WIDTH)


def solution(mesh):
    in_specs = (P("row", "col"), P("row", "col"), P(), P(), P())
    out_specs = P("row", "col")
    return jax.shard_map(shards, mesh=mesh, in_specs=in_specs, out_specs=out_specs, check_vma=False)
```
